32 devices in a mesh: rep: 8 (over y, x, core), tp: 4 (over z).
Axes of the slice: x: 2, y: 2, z: 4, core: 2. Of those that a mesh axis runs over, the one named last changes fastest.
Arguments:
- activations: bfloat16 [8, 8, 257, 1280], P('rep', None, None, 'tp'), may hold values from -6 to 6
- qkv_weight: bfloat16 [8, 3, 1280, 1280], P('rep', None, None, 'tp'), may hold values from -12 to 12
- proj_weight: bfloat16 [8, 1280, 1280], P('rep', 'tp'), may hold values from -0.15625 to 0.15625
- qkv_momentum: float32 [8, 3, 1280, 1280], P('rep', None, None, 'tp'), may hold values from -0.15625 to 0.15625
- proj_momentum: float32 [8, 1280, 1280], P('rep', 'tp'), may hold values from -0.15625 to 0.15625
- head_weight: bfloat16 [8, 1280, 1000], P('rep', None, 'tp'), may hold values from -1.25 to 1.25
- labels: int32 [8, 8], P('rep'), may hold values from 0 to 999
- norm_gain: float32 [1280], replicated, may hold values from 0.25 to 1.75
- head_gain: float32 [1280], replicated, may hold values from 0.25 to 1.75
- gossip_round: int32 [3], replicated, may hold values from 0 to 2, each once
Outputs:
- new_qkv_weight: bfloat16 [8, 3, 1280, 1280], P('rep', None, None, 'tp')
- new_proj_weight: bfloat16 [8, 1280, 1280], P('rep', 'tp')
- new_qkv_momentum: float32 [8, 3, 1280, 1280], P('rep', None, None, 'tp')
- new_proj_momentum: float32 [8, 1280, 1280], P('rep', 'tp')
The draws below stay inside these ranges and needn't reach their ends.
Inputs may be any that keep to these rules, and one draw needn't show every extreme that they name: `gossip_round`: each of 0 to 2 once; the same for all groups.
All inputs are finite; a program needn't handle non-finite values.
Results may differ from the reference program's by a relative error of at most 0.013.
Values may be sent and summed in bfloat16 or wider, within the bound.
A program may use at most 192 MiB of HBM per device.

```python
import jax
import jax.numpy as jnp
from jax import lax

D = 1280
HEADS = 16
HEAD_DIM = 80
S = 257
CLASSES = 1000
IMG = 8
REP = 8
ROUNDS = 3


def draw_qkv_weight(key, part):
    key = jax.random.fold_in(key, 11)
    first_key = jax.random.fold_in(key, 0)
    random_part = jax.random.normal(first_key, (REP, 3, D, HEADS, HEAD_DIM), jnp.float32) * D ** (-0.5)
    return random_part.reshape(REP, 3, D, HEADS * HEAD_DIM).astype(jnp.bfloat16)


def set_ends(array, stream_key, least, top_value):
    shape = array.shape
    spot = [jax.random.randint(jax.random.fold_in(stream_key, axis), (), 0, shape[axis]) for axis in range(len(shape))]
    array = array.at[tuple(spot)].set(least)
    longest = shape.index(max(shape))
    spot[longest] = (spot[longest] + 1) % shape[longest]
    return array.at[tuple(spot)].set(top_value)


def level_of(stream_key, extent, shards, least, high):
    loudness = 1.0
    for position, shards_of in shards:
        heights = jax.random.uniform(jax.random.fold_in(jax.random.fold_in(stream_key, 6), position), (shards_of,), jnp.float32, least / len(shards), high / len(shards))
        loudness = loudness * jnp.repeat(jnp.exp(heights), extent[position] // shards_of).reshape((-1,) + (1,) * (len(extent) - 1 - position))
    return loudness


def noise(stream_key, extent, width, reach, cuts=(), kind=jnp.bfloat16):
    level = level_of(stream_key, extent, cuts, -0.22, 0.18) if cuts else 1.0
    result = jax.random.normal(stream_key, extent, jnp.float32) * width * level
    return jnp.minimum(jnp.maximum(result, -reach), reach).astype(kind)


def setup_inputs(seed: int = 0) -> dict:
    arg_keys = jax.random.split(jax.random.key(seed), 11)
    activations = noise(arg_keys[0], (REP, IMG, S, D), 1.0, 6.0, ((0, 8), (3, 4)))
    qkv_weight = draw_qkv_weight(jax.random.fold_in(arg_keys[10], 71), 0)
    proj_weight = noise(arg_keys[2], (REP, HEADS * HEAD_DIM, D), (HEADS * HEAD_DIM) ** -0.5, 0.15625, ((0, 8), (1, 4)))
    qkv_momentum = noise(arg_keys[3], (REP, 3, D, HEADS * HEAD_DIM), 0.01, 0.15625, ((0, 8), (3, 4)), jnp.float32)
    proj_momentum = noise(arg_keys[4], (REP, HEADS * HEAD_DIM, D), 0.01, 0.15625, ((0, 8), (1, 4)), jnp.float32)
    head_weight = noise(arg_keys[5], (REP, D, CLASSES), 0.084, 1.25, ((0, 8), (2, 4)))
    labels = set_ends(jax.random.randint(arg_keys[6], (REP, IMG), 0, CLASSES), jax.random.fold_in(arg_keys[6], 1), 0, CLASSES - 1).astype(jnp.int32)
    norm_gain = jnp.clip(1.0 + 0.15 * jax.random.normal(arg_keys[7], (D,), jnp.float32), 0.25, 1.75)
    head_gain = jnp.clip(1.0 + 0.15 * jax.random.normal(arg_keys[8], (D,), jnp.float32), 0.25, 1.75)
    gossip_round = jax.random.permutation(arg_keys[9], ROUNDS).astype(jnp.int32)
    return {"activations": activations, "qkv_weight": qkv_weight, "proj_weight": proj_weight, "qkv_momentum": qkv_momentum, "proj_momentum": proj_momentum, "head_weight": head_weight, "labels": labels, "norm_gain": norm_gain, "head_gain": head_gain, "gossip_round": gossip_round}


EPSILON = 1e-06
MOMENTUM = 0.9
LEARNING_RATE = 0.1

def normalize(values, gain):
    average_row = lax.optimization_barrier(jnp.mean(values, axis=-1, keepdims=True))
    centred = values - average_row
    broadcast_copies = lax.optimization_barrier(jnp.mean(centred * centred, axis=-1, keepdims=True))
    inv_std = lax.rsqrt(broadcast_copies + EPSILON)
    unit_rows = centred * inv_std
    return (unit_rows * gain, unit_rows, inv_std)

def softmax_rows(scores):
    row_max = lax.optimization_barrier(jnp.max(scores, axis=-1, keepdims=True))
    raised = jnp.exp(scores - row_max)
    return raised / lax.optimization_barrier(jnp.sum(raised, axis=-1, keepdims=True))

def group_step(activations, qkv_weight, proj_weight, qkv_momentum, proj_momentum, head_weight, labels, norm_gain, head_gain):
    img_count = activations.shape[0]
    tok_count = activations.shape[1]
    feats = HEADS * HEAD_DIM
    score_scale = HEAD_DIM ** (-0.5)
    gathered = activations.astype(jnp.float32)
    normed = normalize(gathered, norm_gain)[0].astype(jnp.bfloat16)
    normalized_row_block = normed.reshape(img_count * tok_count, D)
    projected = [jnp.dot(normalized_row_block, qkv_weight[index], preferred_element_type=jnp.float32).astype(jnp.bfloat16).reshape(img_count, tok_count, HEADS, HEAD_DIM) for index in range(3)]
    queries, key_rows, value_rows = projected
    scores = jnp.einsum('bihe,bjhe->bhij', queries.astype(jnp.float32), key_rows.astype(jnp.float32)) * score_scale
    attend = softmax_rows(scores)
    attend_b = attend.astype(jnp.bfloat16)
    attn_out = jnp.einsum('bhij,bjhe->bihe', attend_b.astype(jnp.float32), value_rows.astype(jnp.float32)).astype(jnp.bfloat16).reshape(img_count, tok_count, feats)
    mixed = gathered + jnp.dot(attn_out.reshape(-1, feats), proj_weight, preferred_element_type=jnp.float32).reshape(img_count, tok_count, D)
    pooled = lax.optimization_barrier(jnp.mean(mixed, axis=1))
    scaled, unit_rows, inv_std = normalize(pooled, head_gain)
    head_in = scaled.astype(jnp.bfloat16)
    logits = jnp.dot(head_in, head_weight, preferred_element_type=jnp.float32)
    class_prob = softmax_rows(logits)
    onehot = (labels[:, None] == jnp.arange(CLASSES, dtype=jnp.int32)[None, :]).astype(jnp.float32)
    logit_grad = (class_prob - onehot).astype(jnp.bfloat16)
    norm_grad = jnp.dot(logit_grad, head_weight.T, preferred_element_type=jnp.float32)
    gain_grad = norm_grad * head_gain
    pool_full = inv_std * (gain_grad - lax.optimization_barrier(jnp.mean(gain_grad, axis=-1, keepdims=True)) - unit_rows * lax.optimization_barrier(jnp.mean(gain_grad * unit_rows, axis=-1, keepdims=True)))
    pool_grad = (pool_full / tok_count).astype(jnp.bfloat16)
    out_sum = lax.optimization_barrier(jnp.sum(attn_out.astype(jnp.float32), axis=1))
    proj_grad = jnp.dot(out_sum.T, pool_grad.astype(jnp.float32), precision=lax.Precision.HIGHEST)
    out_grad = jnp.dot(pool_grad, proj_weight.T, preferred_element_type=jnp.float32).astype(jnp.bfloat16).reshape(img_count, HEADS, HEAD_DIM)
    value_dot = jnp.einsum('bhe,bjhe->bhj', out_grad.astype(jnp.float32), value_rows.astype(jnp.float32))
    row_dot = lax.optimization_barrier(jnp.sum(attend * value_dot[:, :, None, :], axis=-1, keepdims=True))
    score_grad = (attend * (value_dot[:, :, None, :] - row_dot)).astype(jnp.bfloat16)
    query_grad = (jnp.einsum('bhij,bjhe->bihe', score_grad.astype(jnp.float32), key_rows.astype(jnp.float32)) * score_scale).astype(jnp.bfloat16)
    key_grad = (jnp.einsum('bhij,bihe->bjhe', score_grad.astype(jnp.float32), queries.astype(jnp.float32)) * score_scale).astype(jnp.bfloat16)
    column_sum = lax.optimization_barrier(jnp.sum(attend_b.astype(jnp.float32), axis=2))
    value_grad = (jnp.transpose(column_sum, (0, 2, 1))[:, :, :, None] * out_grad.astype(jnp.float32)[:, None, :, :]).astype(jnp.bfloat16)
    query_key_value_gradient = jnp.stack([jnp.dot(normalized_row_block.T, grad_part.reshape(-1, feats), preferred_element_type=jnp.float32) for grad_part in (query_grad, key_grad, value_grad)])
    qkv_new = MOMENTUM * qkv_momentum + query_key_value_gradient
    proj_new = MOMENTUM * proj_momentum + proj_grad
    qkv_step = (qkv_weight.astype(jnp.float32) - LEARNING_RATE * qkv_new).astype(jnp.bfloat16)
    proj_step = (proj_weight.astype(jnp.float32) - LEARNING_RATE * proj_new).astype(jnp.bfloat16)
    return (qkv_step, proj_step, qkv_new, proj_new)

def average_peers(stepped, below, above):
    from_below = jnp.roll(stepped, below, axis=0).astype(jnp.float32)
    from_above = jnp.roll(stepped, -above, axis=0).astype(jnp.float32)
    return ((from_below + stepped.astype(jnp.float32) + from_above) / 3.0).astype(jnp.bfloat16)

def reference(activations, qkv_weight, proj_weight, qkv_momentum, proj_momentum, head_weight, labels, norm_gain, head_gain, gossip_round):

    def one_group(packed):
        return group_step(*packed, norm_gain, head_gain)
    qkv_step, proj_step, qkv_new, proj_new = lax.map(one_group, (activations, qkv_weight, proj_weight, qkv_momentum, proj_momentum, head_weight, labels))
    below = jnp.left_shift(jnp.int32(1), gossip_round[0].astype(jnp.int32))
    above = jnp.left_shift(jnp.int32(1), gossip_round[1].astype(jnp.int32))
    return (average_peers(qkv_step, below, above), average_peers(proj_step, below, above), qkv_new, proj_new)
```

```python
from functools import partial

import jax
import jax.numpy as jnp
from jax import lax
from jax.sharding import PartitionSpec as P

HEAD_DIM = 80


EPSILON = 1e-06
MOMENTUM = 0.9
LEARNING_RATE = 0.1


def from_behind(block, axis, distance):
    devices = range(lax.axis_size(axis))
    route = [((i - distance) % len(devices), i) for i in devices]
    return lax.ppermute(block, axis, route)


def normalize(values, gain):
    average_row = jnp.mean(values, axis=-1, keepdims=True)
    centred = values - average_row
    broadcast_copies = jnp.mean(centred * centred, axis=-1, keepdims=True)
    inv_std = lax.rsqrt(broadcast_copies + EPSILON)
    unit_rows = centred * inv_std
    return (unit_rows * gain, unit_rows, inv_std)


def softmax_rows(scores):
    row_max = jnp.max(scores, axis=-1, keepdims=True)
    raised = jnp.exp(scores - row_max)
    return raised / jnp.sum(raised, axis=-1, keepdims=True)


def average(own_value, from_below, from_above):
    return (
        (
            from_below.astype(jnp.float32)
            + own_value.astype(jnp.float32)
            + from_above.astype(jnp.float32)
        )
        / 3.0
    ).astype(jnp.bfloat16)


def both_ways(payload, below, above):
    return (from_behind_tree(payload, below), from_behind_tree(payload, -above))


def from_behind_tree(payload, distance):
    return jax.tree.map(lambda part: from_behind(part, "rep", distance), payload)


def gossiped(payload, gossip_round):
    count = lax.axis_size("rep").bit_length() - 1
    branches = [
        partial(both_ways, below=1 << first, above=1 << second)
        for first in range(count)
        for second in range(count)
        if second != first
    ]
    first, second = gossip_round[0], gossip_round[1]
    index = first * (count - 1) + second - (second > first).astype(jnp.int32)
    return lax.switch(index, branches, payload)


def on_device(
    activations,
    qkv_weight,
    proj_weight,
    qkv_momentum,
    proj_momentum,
    head_weight,
    labels,
    norm_gain,
    head_gain,
    gossip_round,
):
    local_acts = activations[0]
    img_count, tok_count = (local_acts.shape[0], local_acts.shape[1])
    gathered = lax.all_gather(local_acts, "tp", axis=2, tiled=True)
    full_width = gathered.shape[2]
    gathered_f = gathered.astype(jnp.float32)
    normed = normalize(gathered_f, norm_gain)[0].astype(jnp.bfloat16)
    normalized_row_block = normed.reshape(img_count * tok_count, full_width)
    weight_shard_here = qkv_weight[0]
    local_feats = weight_shard_here.shape[2]
    local_heads = local_feats // HEAD_DIM
    score_scale = HEAD_DIM ** (-0.5)
    projected = jnp.einsum(
        "ai,pie->pae", normalized_row_block, weight_shard_here, preferred_element_type=jnp.float32
    ).astype(jnp.bfloat16)
    queries = projected[0].reshape(img_count, tok_count, local_heads, HEAD_DIM)
    key_rows = projected[1].reshape(img_count, tok_count, local_heads, HEAD_DIM)
    value_rows = projected[2].reshape(img_count, tok_count, local_heads, HEAD_DIM)
    scores = (
        jnp.einsum("bihe,bjhe->bhij", queries, key_rows, preferred_element_type=jnp.float32)
        * score_scale
    )
    attend = softmax_rows(scores)
    attend_b = attend.astype(jnp.bfloat16)
    attn_out = (
        jnp.einsum("bhij,bjhe->bihe", attend_b, value_rows, preferred_element_type=jnp.float32)
        .astype(jnp.bfloat16)
        .reshape(img_count, tok_count, local_feats)
    )
    out_sum = jnp.sum(attn_out.astype(jnp.float32), axis=1)
    proj_local = proj_weight[0]
    pooled_part = jnp.dot(
        out_sum, proj_local.astype(jnp.float32), precision=lax.Precision.HIGHEST
    )
    pooled = jnp.mean(gathered_f, axis=1) + lax.psum(pooled_part, "tp") / tok_count
    scaled, unit_rows, inv_std = normalize(pooled, head_gain)
    head_in = scaled.astype(jnp.bfloat16)
    head_local = head_weight[0]
    local_classes = head_local.shape[1]
    logits = jnp.dot(head_in, head_local, preferred_element_type=jnp.float32)
    row_max = jnp.max(logits, axis=-1, keepdims=True)
    row_total = jnp.sum(jnp.exp(logits - row_max), axis=-1, keepdims=True)
    stats = lax.all_gather(jnp.concatenate([row_max, row_total], axis=1), "tp")
    merged_max = jnp.max(stats[:, :, :1], axis=0)
    merged_total = jnp.sum(stats[:, :, 1:] * jnp.exp(stats[:, :, :1] - merged_max), axis=0)
    class_prob = jnp.exp(logits - merged_max) / merged_total
    class_start = lax.axis_index("tp") * local_classes
    onehot = (
        labels[0][:, None] == class_start + jnp.arange(local_classes, dtype=jnp.int32)[None, :]
    ).astype(jnp.float32)
    logit_grad = (class_prob - onehot).astype(jnp.bfloat16)
    norm_part = jnp.dot(logit_grad, head_local.T, preferred_element_type=jnp.float32)
    norm_grad = lax.psum(norm_part, "tp")
    gain_grad = norm_grad * head_gain
    pool_full = inv_std * (
        gain_grad
        - jnp.mean(gain_grad, axis=-1, keepdims=True)
        - unit_rows * jnp.mean(gain_grad * unit_rows, axis=-1, keepdims=True)
    )
    pool_grad = (pool_full / tok_count).astype(jnp.bfloat16)
    proj_grad = jnp.dot(out_sum.T, pool_grad.astype(jnp.float32), precision=lax.Precision.HIGHEST)
    proj_new = MOMENTUM * proj_momentum[0] + proj_grad
    proj_step = (proj_local.astype(jnp.float32) - LEARNING_RATE * proj_new).astype(jnp.bfloat16)[
        None
    ]
    out_grad = (
        jnp.dot(pool_grad, proj_local.T, preferred_element_type=jnp.float32)
        .astype(jnp.bfloat16)
        .reshape(img_count, local_heads, HEAD_DIM)
    )
    value_dot = jnp.einsum(
        "bhe,bjhe->bhj", out_grad, value_rows, preferred_element_type=jnp.float32
    )
    row_dot = jnp.sum(attend * value_dot[:, :, None, :], axis=-1, keepdims=True)
    score_grad = (attend * (value_dot[:, :, None, :] - row_dot)).astype(jnp.bfloat16)
    query_grad = (
        jnp.einsum("bhij,bjhe->bihe", score_grad, key_rows, preferred_element_type=jnp.float32)
        * score_scale
    ).astype(jnp.bfloat16)
    key_grad = (
        jnp.einsum("bhij,bihe->bjhe", score_grad, queries, preferred_element_type=jnp.float32)
        * score_scale
    ).astype(jnp.bfloat16)
    column_sum = jnp.sum(attend_b.astype(jnp.float32), axis=2)
    value_grad = (
        jnp.transpose(column_sum, (0, 2, 1))[:, :, :, None]
        * out_grad.astype(jnp.float32)[:, None, :, :]
    ).astype(jnp.bfloat16)
    stacked_arrays = jnp.stack(
        [
            query_grad.reshape(-1, local_feats),
            key_grad.reshape(-1, local_feats),
            value_grad.reshape(-1, local_feats),
        ]
    )
    query_key_value_gradient = jnp.einsum(
        "sw,ksl->kwl", normalized_row_block, stacked_arrays, preferred_element_type=jnp.float32
    )
    qkv_new = MOMENTUM * qkv_momentum[0] + query_key_value_gradient
    qkv_step = (weight_shard_here.astype(jnp.float32) - LEARNING_RATE * qkv_new).astype(
        jnp.bfloat16
    )[None]
    from_below, from_above = gossiped((qkv_step, proj_step), gossip_round)
    qkv_avg = average(qkv_step, from_below[0], from_above[0])
    projection_mean = average(proj_step, from_below[1], from_above[1])
    return (qkv_avg, projection_mean, qkv_new[None], proj_new[None])


def solution(mesh):
    return jax.shard_map(
        on_device,
        mesh=mesh,
        in_specs=(
            P("rep", None, None, "tp"),
            P("rep", None, None, "tp"),
            P("rep", "tp", None),
            P("rep", None, None, "tp"),
            P("rep", "tp", None),
            P("rep", None, "tp"),
            P("rep", None),
            P(),
            P(),
            P(),
        ),
        out_specs=(
            P("rep", None, None, "tp"),
            P("rep", "tp", None),
            P("rep", None, None, "tp"),
            P("rep", "tp", None),
        ),
        check_vma=False,
    )
```

```python
from functools import partial

import jax
import jax.numpy as jnp
from jax import lax
from jax.experimental import pallas as pl
from jax.experimental.pallas import tpu as pltpu
from jax.sharding import PartitionSpec as P

HEAD_DIM = 80


EPSILON = 1e-06
MOMENTUM = 0.9
LEARNING_RATE = 0.1


def from_behind(block, axis, distance):
    devices = range(lax.axis_size(axis))
    route = [((i - distance) % len(devices), i) for i in devices]
    return lax.ppermute(block, axis, route)


def normalize(values, gain):
    average_row = jnp.mean(values, axis=-1, keepdims=True)
    centred = values - average_row
    broadcast_copies = jnp.mean(centred * centred, axis=-1, keepdims=True)
    inv_std = lax.rsqrt(broadcast_copies + EPSILON)
    unit_rows = centred * inv_std
    return (unit_rows * gain, unit_rows, inv_std)


def average(own_value, from_below, from_above):
    return (
        (
            from_below.astype(jnp.float32)
            + own_value.astype(jnp.float32)
            + from_above.astype(jnp.float32)
        )
        / 3.0
    ).astype(jnp.bfloat16)


def both_ways(payload, below, above):
    return (from_behind_tree(payload, below), from_behind_tree(payload, -above))


def from_behind_tree(payload, distance):
    return jax.tree.map(lambda part: from_behind(part, "rep", distance), payload)


def gossiped(payload, gossip_round):
    count = lax.axis_size("rep").bit_length() - 1
    branches = [
        partial(both_ways, below=1 << first, above=1 << second)
        for first in range(count)
        for second in range(count)
        if second != first
    ]
    first, second = gossip_round[0], gossip_round[1]
    index = first * (count - 1) + second - (second > first).astype(jnp.int32)
    return lax.switch(index, branches, payload)


def head_mask(head, shape):
    lane = lax.broadcasted_iota(jnp.int32, shape, 1)
    return (lane >= head * HEAD_DIM) & (lane < (head + 1) * HEAD_DIM)


def scores_by_key(queries, key_rows, head):
    picked = jnp.where(head_mask(head, queries.shape), queries, jnp.zeros_like(queries))
    return lax.dot_general(
        key_rows, picked, (((1,), (1,)), ((), ())), preferred_element_type=jnp.float32
    ) * (HEAD_DIM ** (-0.5))


def forward_kernel(
    tok_count,
    x_ref,
    w_ref,
    gain_ref,
    normed_ref,
    qkv_ref,
    lse_ref,
    weight_sum_ref,
    out_sum_ref,
    x_sum_ref,
    tokens,
    send_sem,
    pass_sem,
    recv_sem,
):
    shards = tokens.shape[0]
    pairs = tokens.shape[1]
    rows = tokens.shape[3]
    local_feats = x_ref.shape[2]
    local_heads = local_feats // HEAD_DIM
    full_width = shards * local_feats
    me = lax.axis_index("tp")

    barrier = pltpu.get_barrier_semaphore()
    for step in range(1, shards):
        pl.semaphore_signal(
            barrier,
            inc=1,
            device_id={"tp": lax.rem(me + step, shards)},
            device_id_type=pl.DeviceIdType.MESH,
        )
    pl.semaphore_wait(barrier, shards - 1)

    def copy_of(source, pair, target, sem):
        return pltpu.make_async_remote_copy(
            src_ref=tokens.at[source, pair],
            dst_ref=tokens.at[source, pair],
            send_sem=sem,
            recv_sem=recv_sem.at[source, pair],
            device_id={"tp": target},
            device_id_type=pl.DeviceIdType.MESH,
        )

    def send(pair):
        even = x_ref[2 * pair]
        odd = x_ref[2 * pair + 1]
        tokens[me, pair, 0] = even[:, :128]
        tokens[me, pair, 1] = even[:, 128:256]
        tokens[me, pair, 2] = odd[:, :128]
        tokens[me, pair, 3] = odd[:, 128:256]
        tokens[me, pair, 4] = jnp.concatenate([even[:, 256:], odd[:, 256:]], axis=1)
        for distance in (2, -2, 1, -1):
            target = me + distance

            @pl.when((target >= 0) & (target < shards))
            def _():
                copy_of(me, pair, target, send_sem.at[distance + 2, pair]).start()

    send(0)
    send(1)
    valid = lax.broadcasted_iota(jnp.int32, (rows, rows), 0) < tok_count
    passer = (me == 1) | (me == 2)
    passed = jnp.where(me == 1, 3, 0)
    passed_to = jnp.where(me == 1, 0, 3)

    def one_pair(pair, carry):
        @pl.when(passer)
        def _():
            copy_of(passed, pair, passed_to, pass_sem.at[pair]).wait_recv()
            copy_of(passed, pair, passed_to, pass_sem.at[pair]).start()

        for source in range(shards):

            @pl.when((source != me) & ~(passer & (source == passed)))
            def _():
                copy_of(source, pair, source, pass_sem.at[pair]).wait_recv()

        @pl.when(pair + 2 < pairs)
        def _():
            send(pair + 2)

        for parity in range(2):
            img = 2 * pair + parity
            parts = []
            for source in range(shards):
                tail = tokens[source, pair, 4]
                parts.append(
                    jnp.concatenate(
                        [
                            tokens[source, pair, 2 * parity],
                            tokens[source, pair, 2 * parity + 1],
                            tail[:, 64 * parity : 64 * parity + 64],
                        ],
                        axis=1,
                    ).astype(jnp.float32)
                )
            average_row = sum(jnp.sum(part, axis=1, keepdims=True) for part in parts) / full_width
            spread = (
                sum(
                    jnp.sum((part - average_row) * (part - average_row), axis=1, keepdims=True)
                    for part in parts
                )
                / full_width
            )
            inv_std = lax.rsqrt(spread + EPSILON)
            projected = [None] * 3
            for source in range(shards):
                normed = ((parts[source] - average_row) * inv_std * gain_ref[source]).astype(
                    jnp.bfloat16
                )
                normed_ref[source, img] = normed
                x_sum_ref[img, source] = jnp.sum(parts[source], axis=0, keepdims=True)
                for kind in range(3):
                    piece = jnp.dot(
                        normed,
                        w_ref[kind, source * local_feats : (source + 1) * local_feats, :],
                        preferred_element_type=jnp.float32,
                    )
                    projected[kind] = piece if source == 0 else projected[kind] + piece
            queries, key_rows, value_rows = [part.astype(jnp.bfloat16) for part in projected]
            qkv_ref[0, img] = queries
            qkv_ref[1, img] = key_rows
            qkv_ref[2, img] = value_rows
            weight_sum = jnp.zeros((rows, local_feats), jnp.float32)
            token = lax.broadcasted_iota(jnp.int32, (rows, local_feats), 0) < tok_count
            for head in range(local_heads):
                scores = scores_by_key(queries, key_rows, head)
                scores = jnp.where(valid, scores, -1e30)
                top = jnp.max(scores, axis=0, keepdims=True)
                raised = jnp.exp(scores - top)
                total = jnp.sum(raised, axis=0, keepdims=True)
                attend = (raised / total).astype(jnp.bfloat16)
                lse_ref[img, head : head + 1] = top + jnp.log(total)
                picked = (token & head_mask(head, (rows, local_feats))).astype(jnp.bfloat16)
                weight_sum = weight_sum + jnp.dot(
                    attend, picked, preferred_element_type=jnp.float32
                )
            weight_sum_ref[img] = weight_sum
            out_sum_ref[img] = jnp.sum(
                weight_sum * value_rows.astype(jnp.float32), axis=0, keepdims=True
            )
        return carry

    lax.fori_loop(0, pairs, one_pair, 0)

    def finish(pair, carry):
        for distance in (2, -2, 1, -1):
            target = me + distance

            @pl.when((target >= 0) & (target < shards))
            def _():
                copy_of(me, pair, target, send_sem.at[distance + 2, pair]).wait_send()

        @pl.when(passer)
        def _():
            copy_of(passed, pair, passed_to, pass_sem.at[pair]).wait_send()

        return carry

    lax.fori_loop(0, pairs, finish, 0)


def forward(local_acts, weight_shard, norm_gain):
    img_count, tok_count, local_feats = local_acts.shape
    shards = lax.axis_size("tp")
    rows = -(-tok_count // 16) * 16
    pairs = img_count // 2
    padded = jnp.pad(local_acts, ((0, 0), (0, rows - tok_count), (0, 0)))
    gain = norm_gain.reshape(shards, 1, local_feats)
    shapes = [
        jax.ShapeDtypeStruct((shards, img_count, rows, local_feats), jnp.bfloat16),
        jax.ShapeDtypeStruct((3, img_count, rows, local_feats), jnp.bfloat16),
        jax.ShapeDtypeStruct((img_count, 8, rows), jnp.float32),
        jax.ShapeDtypeStruct((img_count, rows, local_feats), jnp.float32),
        jax.ShapeDtypeStruct((img_count, 1, local_feats), jnp.float32),
        jax.ShapeDtypeStruct((img_count, shards, 1, local_feats), jnp.float32),
    ]
    return pl.pallas_call(
        partial(forward_kernel, tok_count),
        out_shape=shapes,
        in_specs=[pl.BlockSpec(memory_space=pltpu.VMEM)] * 3,
        out_specs=[pl.BlockSpec(memory_space=pltpu.VMEM)] * len(shapes),
        scratch_shapes=[
            pltpu.VMEM((shards, pairs, 5, rows, 128), jnp.bfloat16),
            pltpu.SemaphoreType.DMA((5, pairs)),
            pltpu.SemaphoreType.DMA((pairs,)),
            pltpu.SemaphoreType.DMA((shards, pairs)),
        ],
        compiler_params=pltpu.CompilerParams(
            collective_id=0, has_side_effects=True, vmem_limit_bytes=56 * 1024 * 1024
        ),
    )(padded, weight_shard, gain)


def backward_kernel(tok_count, qkv_ref, lse_ref, weight_sum_ref, out_grad_ref, grad_ref):
    queries, key_rows, value_rows = qkv_ref[0, 0], qkv_ref[1, 0], qkv_ref[2, 0]
    rows, local_feats = queries.shape
    local_heads = local_feats // HEAD_DIM
    out_grad = out_grad_ref[0].astype(jnp.float32)
    valid = lax.broadcasted_iota(jnp.int32, (rows, rows), 0) < tok_count
    weighed = value_rows.astype(jnp.float32) * out_grad
    query_grad = jnp.zeros((rows, local_feats), jnp.float32)
    key_grad = jnp.zeros((rows, local_feats), jnp.float32)
    for head in range(local_heads):
        mask = head_mask(head, (rows, local_feats))
        scores = scores_by_key(queries, key_rows, head)
        attend = jnp.where(valid, jnp.exp(scores - lse_ref[0, head : head + 1]), 0.0)
        value_dot = jnp.sum(jnp.where(mask, weighed, 0.0), axis=1, keepdims=True)
        row_dot = jnp.sum(attend * value_dot, axis=0, keepdims=True)
        score_grad = (attend * (value_dot - row_dot)).astype(jnp.bfloat16)
        key_grad = key_grad + jnp.dot(
            score_grad,
            jnp.where(mask, queries, jnp.zeros_like(queries)),
            preferred_element_type=jnp.float32,
        )
        query_grad = query_grad + lax.dot_general(
            score_grad,
            jnp.where(mask, key_rows, jnp.zeros_like(key_rows)),
            (((0,), (0,)), ((), ())),
            preferred_element_type=jnp.float32,
        )
    scale = HEAD_DIM ** (-0.5)
    grad_ref[0, 0] = (query_grad * scale).astype(jnp.bfloat16)
    grad_ref[1, 0] = (key_grad * scale).astype(jnp.bfloat16)
    grad_ref[2, 0] = (weight_sum_ref[0] * out_grad).astype(jnp.bfloat16)


def backward(tok_count, qkv, lse, weight_sum, out_grad):
    _, img_count, rows, local_feats = qkv.shape
    return pl.pallas_call(
        partial(backward_kernel, tok_count),
        grid=(img_count,),
        out_shape=jax.ShapeDtypeStruct(qkv.shape, jnp.bfloat16),
        in_specs=[
            pl.BlockSpec((3, 1, rows, local_feats), lambda i: (0, i, 0, 0)),
            pl.BlockSpec((1, 8, rows), lambda i: (i, 0, 0)),
            pl.BlockSpec((1, rows, local_feats), lambda i: (i, 0, 0)),
            pl.BlockSpec((1, 1, local_feats), lambda i: (i, 0, 0)),
        ],
        out_specs=pl.BlockSpec((3, 1, rows, local_feats), lambda i: (0, i, 0, 0)),
        compiler_params=pltpu.CompilerParams(vmem_limit_bytes=48 * 1024 * 1024),
    )(qkv, lse, weight_sum, out_grad[:, None])


def on_device(
    activations,
    qkv_weight,
    proj_weight,
    qkv_momentum,
    proj_momentum,
    head_weight,
    labels,
    norm_gain,
    head_gain,
    gossip_round,
):
    local_acts = activations[0]
    img_count, tok_count = (local_acts.shape[0], local_acts.shape[1])
    weight_shard_here = qkv_weight[0]
    local_feats = weight_shard_here.shape[2]
    full_width = weight_shard_here.shape[1]
    normed, qkv, lse, weight_sum, out_sum, x_sum = forward(
        local_acts, weight_shard_here, norm_gain
    )
    out_sum = out_sum.reshape(img_count, local_feats)
    x_sum = x_sum.reshape(img_count, full_width)
    proj_local = proj_weight[0]
    pooled_part = jnp.dot(
        out_sum, proj_local.astype(jnp.float32), precision=lax.Precision.HIGHEST
    )
    pooled = (x_sum + lax.psum(pooled_part, "tp")) / tok_count
    scaled, unit_rows, inv_std = normalize(pooled, head_gain)
    head_in = scaled.astype(jnp.bfloat16)
    head_local = head_weight[0]
    local_classes = head_local.shape[1]
    logits = jnp.dot(head_in, head_local, preferred_element_type=jnp.float32)
    row_max = jnp.max(logits, axis=-1, keepdims=True)
    row_total = jnp.sum(jnp.exp(logits - row_max), axis=-1, keepdims=True)
    stats = lax.all_gather(jnp.concatenate([row_max, row_total], axis=1), "tp")
    merged_max = jnp.max(stats[:, :, :1], axis=0)
    merged_total = jnp.sum(stats[:, :, 1:] * jnp.exp(stats[:, :, :1] - merged_max), axis=0)
    class_prob = jnp.exp(logits - merged_max) / merged_total
    class_start = lax.axis_index("tp") * local_classes
    onehot = (
        labels[0][:, None] == class_start + jnp.arange(local_classes, dtype=jnp.int32)[None, :]
    ).astype(jnp.float32)
    logit_grad = (class_prob - onehot).astype(jnp.bfloat16)
    norm_part = jnp.dot(logit_grad, head_local.T, preferred_element_type=jnp.float32)
    norm_grad = lax.psum(norm_part, "tp")
    gain_grad = norm_grad * head_gain
    pool_full = inv_std * (
        gain_grad
        - jnp.mean(gain_grad, axis=-1, keepdims=True)
        - unit_rows * jnp.mean(gain_grad * unit_rows, axis=-1, keepdims=True)
    )
    pool_grad = (pool_full / tok_count).astype(jnp.bfloat16)
    proj_grad = jnp.dot(out_sum.T, pool_grad.astype(jnp.float32), precision=lax.Precision.HIGHEST)
    proj_new = MOMENTUM * proj_momentum[0] + proj_grad
    proj_step = (proj_local.astype(jnp.float32) - LEARNING_RATE * proj_new).astype(jnp.bfloat16)[
        None
    ]
    out_grad = jnp.dot(pool_grad, proj_local.T, preferred_element_type=jnp.float32).astype(
        jnp.bfloat16
    )
    stacked_arrays = backward(tok_count, qkv, lse, weight_sum, out_grad)
    query_key_value_gradient = jnp.einsum(
        "sbiw,kbil->kswl", normed, stacked_arrays, preferred_element_type=jnp.float32
    ).reshape(3, full_width, local_feats)
    qkv_new = MOMENTUM * qkv_momentum[0] + query_key_value_gradient
    qkv_step = (weight_shard_here.astype(jnp.float32) - LEARNING_RATE * qkv_new).astype(
        jnp.bfloat16
    )[None]
    from_below, from_above = gossiped((qkv_step, proj_step), gossip_round)
    qkv_avg = average(qkv_step, from_below[0], from_above[0])
    projection_mean = average(proj_step, from_below[1], from_above[1])
    return (qkv_avg, projection_mean, qkv_new[None], proj_new[None])


def solution(mesh):
    return jax.shard_map(
        on_device,
        mesh=mesh,
        in_specs=(
            P("rep", None, None, "tp"),
            P("rep", None, None, "tp"),
            P("rep", "tp", None),
            P("rep", None, None, "tp"),
            P("rep", "tp", None),
            P("rep", None, "tp"),
            P("rep", None),
            P(),
            P(),
            P(),
        ),
        out_specs=(
            P("rep", None, None, "tp"),
            P("rep", "tp", None),
            P("rep", None, None, "tp"),
            P("rep", "tp", None),
        ),
        check_vma=False,
    )
```

```python
from functools import partial

import jax
import jax.numpy as jnp
from jax import lax
from jax.experimental import pallas as pl
from jax.experimental.pallas import tpu as pltpu
from jax.sharding import PartitionSpec as P

HEAD_DIM = 80


EPSILON = 1e-06
MOMENTUM = 0.9
LEARNING_RATE = 0.1


def from_behind(block, axis, distance):
    devices = range(lax.axis_size(axis))
    route = [((i - distance) % len(devices), i) for i in devices]
    return lax.ppermute(block, axis, route)


def normalize(values, gain):
    average_row = jnp.mean(values, axis=-1, keepdims=True)
    centred = values - average_row
    broadcast_copies = jnp.mean(centred * centred, axis=-1, keepdims=True)
    inv_std = lax.rsqrt(broadcast_copies + EPSILON)
    unit_rows = centred * inv_std
    return (unit_rows * gain, unit_rows, inv_std)


def average(own_value, from_below, from_above):
    return (
        (
            from_below.astype(jnp.float32)
            + own_value.astype(jnp.float32)
            + from_above.astype(jnp.float32)
        )
        / 3.0
    ).astype(jnp.bfloat16)


def gossiped(work, operands, gossip_round):
    count = lax.axis_size("rep").bit_length() - 1
    branches = [
        partial(work, below=1 << first, above=1 << second)
        for first in range(count)
        for second in range(count)
        if second != first
    ]
    first, second = gossip_round[0], gossip_round[1]
    index = first * (count - 1) + second - (second > first).astype(jnp.int32)
    return lax.switch(index, branches, operands)


def stepped(normed, grad, momentum, weight):
    product = jnp.einsum("sbiw,bil->swl", normed, grad, preferred_element_type=jnp.float32)
    new = MOMENTUM * momentum + product.reshape(momentum.shape)
    return new, (weight.astype(jnp.float32) - LEARNING_RATE * new).astype(jnp.bfloat16)


def head_mask(head, shape):
    lane = lax.broadcasted_iota(jnp.int32, shape, 1)
    return (lane >= head * HEAD_DIM) & (lane < (head + 1) * HEAD_DIM)


def scores_by_key(queries, key_rows, head):
    picked = jnp.where(head_mask(head, queries.shape), queries, jnp.zeros_like(queries))
    return lax.dot_general(
        key_rows, picked, (((1,), (1,)), ((), ())), preferred_element_type=jnp.float32
    ) * (HEAD_DIM ** (-0.5))


def forward_kernel(
    tok_count,
    x_ref,
    w_ref,
    gain_ref,
    normed_ref,
    qkv_ref,
    lse_ref,
    weight_sum_ref,
    out_sum_ref,
    x_sum_ref,
    tokens,
    send_sem,
    pass_sem,
    recv_sem,
):
    shards = tokens.shape[0]
    pairs = tokens.shape[1]
    rows = tokens.shape[3]
    local_feats = x_ref.shape[2]
    local_heads = local_feats // HEAD_DIM
    full_width = shards * local_feats
    me = lax.axis_index("tp")

    barrier = pltpu.get_barrier_semaphore()
    for step in range(1, shards):
        pl.semaphore_signal(
            barrier,
            inc=1,
            device_id={"tp": lax.rem(me + step, shards)},
            device_id_type=pl.DeviceIdType.MESH,
        )
    pl.semaphore_wait(barrier, shards - 1)

    def copy_of(source, pair, target, sem):
        return pltpu.make_async_remote_copy(
            src_ref=tokens.at[source, pair],
            dst_ref=tokens.at[source, pair],
            send_sem=sem,
            recv_sem=recv_sem.at[source, pair],
            device_id={"tp": target},
            device_id_type=pl.DeviceIdType.MESH,
        )

    def send(pair):
        even = x_ref[2 * pair]
        odd = x_ref[2 * pair + 1]
        tokens[me, pair, 0] = even[:, :128]
        tokens[me, pair, 1] = even[:, 128:256]
        tokens[me, pair, 2] = odd[:, :128]
        tokens[me, pair, 3] = odd[:, 128:256]
        tokens[me, pair, 4] = jnp.concatenate([even[:, 256:], odd[:, 256:]], axis=1)
        for distance in (2, -2, 1, -1):
            target = me + distance

            @pl.when((target >= 0) & (target < shards))
            def _():
                copy_of(me, pair, target, send_sem.at[distance + 2, pair]).start()

    send(0)
    send(1)
    valid = lax.broadcasted_iota(jnp.int32, (rows, rows), 0) < tok_count
    passer = (me == 1) | (me == 2)
    passed = jnp.where(me == 1, 3, 0)
    passed_to = jnp.where(me == 1, 0, 3)

    def one_pair(pair, carry):
        @pl.when(passer)
        def _():
            copy_of(passed, pair, passed_to, pass_sem.at[pair]).wait_recv()
            copy_of(passed, pair, passed_to, pass_sem.at[pair]).start()

        for source in range(shards):

            @pl.when((source != me) & ~(passer & (source == passed)))
            def _():
                copy_of(source, pair, source, pass_sem.at[pair]).wait_recv()

        @pl.when(pair + 2 < pairs)
        def _():
            send(pair + 2)

        for parity in range(2):
            img = 2 * pair + parity
            parts = []
            for source in range(shards):
                tail = tokens[source, pair, 4]
                parts.append(
                    jnp.concatenate(
                        [
                            tokens[source, pair, 2 * parity],
                            tokens[source, pair, 2 * parity + 1],
                            tail[:, 64 * parity : 64 * parity + 64],
                        ],
                        axis=1,
                    ).astype(jnp.float32)
                )
            average_row = sum(jnp.sum(part, axis=1, keepdims=True) for part in parts) / full_width
            spread = (
                sum(
                    jnp.sum((part - average_row) * (part - average_row), axis=1, keepdims=True)
                    for part in parts
                )
                / full_width
            )
            inv_std = lax.rsqrt(spread + EPSILON)
            projected = [None] * 3
            for source in range(shards):
                normed = ((parts[source] - average_row) * inv_std * gain_ref[source]).astype(
                    jnp.bfloat16
                )
                normed_ref[source, img] = normed
                x_sum_ref[img, source] = jnp.sum(parts[source], axis=0, keepdims=True)
                for kind in range(3):
                    piece = jnp.dot(
                        normed,
                        w_ref[kind, source * local_feats : (source + 1) * local_feats, :],
                        preferred_element_type=jnp.float32,
                    )
                    projected[kind] = piece if source == 0 else projected[kind] + piece
            queries, key_rows, value_rows = [part.astype(jnp.bfloat16) for part in projected]
            qkv_ref[0, img] = queries
            qkv_ref[1, img] = key_rows
            qkv_ref[2, img] = value_rows
            weight_sum = jnp.zeros((rows, local_feats), jnp.float32)
            token = lax.broadcasted_iota(jnp.int32, (rows, local_feats), 0) < tok_count
            for head in range(local_heads):
                scores = scores_by_key(queries, key_rows, head)
                scores = jnp.where(valid, scores, -1e30)
                top = jnp.max(scores, axis=0, keepdims=True)
                raised = jnp.exp(scores - top)
                total = jnp.sum(raised, axis=0, keepdims=True)
                attend = (raised / total).astype(jnp.bfloat16)
                lse_ref[img, head : head + 1] = top + jnp.log(total)
                picked = (token & head_mask(head, (rows, local_feats))).astype(jnp.bfloat16)
                weight_sum = weight_sum + jnp.dot(
                    attend, picked, preferred_element_type=jnp.float32
                )
            weight_sum_ref[img] = weight_sum
            out_sum_ref[img] = jnp.sum(
                weight_sum * value_rows.astype(jnp.float32), axis=0, keepdims=True
            )
        return carry

    lax.fori_loop(0, pairs, one_pair, 0)

    def finish(pair, carry):
        for distance in (2, -2, 1, -1):
            target = me + distance

            @pl.when((target >= 0) & (target < shards))
            def _():
                copy_of(me, pair, target, send_sem.at[distance + 2, pair]).wait_send()

        @pl.when(passer)
        def _():
            copy_of(passed, pair, passed_to, pass_sem.at[pair]).wait_send()

        return carry

    lax.fori_loop(0, pairs, finish, 0)


def forward(local_acts, weight_shard, norm_gain):
    img_count, tok_count, local_feats = local_acts.shape
    shards = lax.axis_size("tp")
    rows = -(-tok_count // 16) * 16
    pairs = img_count // 2
    padded = jnp.pad(local_acts, ((0, 0), (0, rows - tok_count), (0, 0)))
    gain = norm_gain.reshape(shards, 1, local_feats)
    shapes = [
        jax.ShapeDtypeStruct((shards, img_count, rows, local_feats), jnp.bfloat16),
        jax.ShapeDtypeStruct((3, img_count, rows, local_feats), jnp.bfloat16),
        jax.ShapeDtypeStruct((img_count, 8, rows), jnp.float32),
        jax.ShapeDtypeStruct((img_count, rows, local_feats), jnp.float32),
        jax.ShapeDtypeStruct((img_count, 1, local_feats), jnp.float32),
        jax.ShapeDtypeStruct((img_count, shards, 1, local_feats), jnp.float32),
    ]
    return pl.pallas_call(
        partial(forward_kernel, tok_count),
        out_shape=shapes,
        in_specs=[pl.BlockSpec(memory_space=pltpu.VMEM)] * 3,
        out_specs=[pl.BlockSpec(memory_space=pltpu.VMEM)] * len(shapes),
        scratch_shapes=[
            pltpu.VMEM((shards, pairs, 5, rows, 128), jnp.bfloat16),
            pltpu.SemaphoreType.DMA((5, pairs)),
            pltpu.SemaphoreType.DMA((pairs,)),
            pltpu.SemaphoreType.DMA((shards, pairs)),
        ],
        compiler_params=pltpu.CompilerParams(
            collective_id=0, has_side_effects=True, vmem_limit_bytes=56 * 1024 * 1024
        ),
    )(padded, weight_shard, gain)


def backward_kernel(tok_count, qkv_ref, lse_ref, out_grad_ref, grad_ref):
    queries, key_rows, value_rows = qkv_ref[0, 0], qkv_ref[1, 0], qkv_ref[2, 0]
    rows, local_feats = queries.shape
    local_heads = local_feats // HEAD_DIM
    out_grad = out_grad_ref[0].astype(jnp.float32)
    valid = lax.broadcasted_iota(jnp.int32, (rows, rows), 0) < tok_count
    weighed = value_rows.astype(jnp.float32) * out_grad
    query_grad = jnp.zeros((rows, local_feats), jnp.float32)
    key_grad = jnp.zeros((rows, local_feats), jnp.float32)
    for head in range(local_heads):
        mask = head_mask(head, (rows, local_feats))
        scores = scores_by_key(queries, key_rows, head)
        attend = jnp.where(valid, jnp.exp(scores - lse_ref[0, head : head + 1]), 0.0)
        value_dot = jnp.sum(jnp.where(mask, weighed, 0.0), axis=1, keepdims=True)
        row_dot = jnp.sum(attend * value_dot, axis=0, keepdims=True)
        score_grad = (attend * (value_dot - row_dot)).astype(jnp.bfloat16)
        key_grad = key_grad + jnp.dot(
            score_grad,
            jnp.where(mask, queries, jnp.zeros_like(queries)),
            preferred_element_type=jnp.float32,
        )
        query_grad = query_grad + lax.dot_general(
            score_grad,
            jnp.where(mask, key_rows, jnp.zeros_like(key_rows)),
            (((0,), (0,)), ((), ())),
            preferred_element_type=jnp.float32,
        )
    scale = HEAD_DIM ** (-0.5)
    grad_ref[0, 0] = (query_grad * scale).astype(jnp.bfloat16)
    grad_ref[1, 0] = (key_grad * scale).astype(jnp.bfloat16)


def backward(tok_count, qkv, lse, out_grad):
    _, img_count, rows, local_feats = qkv.shape
    return pl.pallas_call(
        partial(backward_kernel, tok_count),
        grid=(img_count,),
        out_shape=jax.ShapeDtypeStruct((2,) + qkv.shape[1:], jnp.bfloat16),
        in_specs=[
            pl.BlockSpec((3, 1, rows, local_feats), lambda i: (0, i, 0, 0)),
            pl.BlockSpec((1, 8, rows), lambda i: (i, 0, 0)),
            pl.BlockSpec((1, 1, local_feats), lambda i: (i, 0, 0)),
        ],
        out_specs=pl.BlockSpec((2, 1, rows, local_feats), lambda i: (0, i, 0, 0)),
        cost_estimate=pl.CostEstimate(
            flops=20_000_000_000, bytes_accessed=16_000_000, transcendentals=4_000_000
        ),
        compiler_params=pltpu.CompilerParams(vmem_limit_bytes=48 * 1024 * 1024),
    )(qkv, lse, out_grad[:, None])


def thirds(values):
    high = values.astype(jnp.bfloat16).astype(jnp.float32)
    middle = (values - high).astype(jnp.bfloat16).astype(jnp.float32)
    return [high, middle, values - high - middle]


def head_kernel(
    tok_count,
    out_sum_ref,
    x_sum_ref,
    proj_ref,
    head_ref,
    onehot_ref,
    gain_ref,
    pool_grad_ref,
    out_grad_ref,
    pooled_parts,
    grad_parts,
    send_sem,
    recv_sem,
):
    shards = pooled_parts.shape[0]
    imgs, full_width = x_sum_ref.shape
    me = lax.axis_index("tp")

    barrier = pltpu.get_barrier_semaphore()
    for step in range(1, shards):
        pl.semaphore_signal(
            barrier,
            inc=1,
            device_id={"tp": lax.rem(me + step, shards)},
            device_id_type=pl.DeviceIdType.MESH,
        )

    def exchange(parts, turn):
        copies = [
            pltpu.make_async_remote_copy(
                src_ref=parts.at[me],
                dst_ref=parts.at[me],
                send_sem=send_sem.at[turn, step],
                recv_sem=recv_sem.at[turn, step],
                device_id={"tp": lax.rem(me + step, shards)},
                device_id_type=pl.DeviceIdType.MESH,
            )
            for step in range(1, shards)
        ]
        for copy in copies:
            copy.start()
        for copy in copies:
            copy.wait()

    split = jnp.concatenate(thirds(out_sum_ref[...]), axis=0).astype(jnp.bfloat16)
    product = jnp.dot(split, proj_ref[...], preferred_element_type=jnp.float32)
    pooled_parts[me] = product[:imgs] + product[imgs : 2 * imgs] + product[2 * imgs :]
    pl.semaphore_wait(barrier, shards - 1)
    exchange(pooled_parts, 0)
    pooled = x_sum_ref[...]
    for source in range(shards):
        pooled = pooled + pooled_parts[source]
    pooled = pooled / tok_count
    gain = gain_ref[...]
    scaled, unit_rows, inv_std = normalize(pooled, gain)
    logits = jnp.dot(
        scaled.astype(jnp.bfloat16), head_ref[...], preferred_element_type=jnp.float32
    )
    row_max = jnp.max(logits, axis=1, keepdims=True)
    raised = jnp.exp(logits - row_max)
    row_total = jnp.sum(raised, axis=1, keepdims=True)
    stacked = jnp.concatenate(thirds(raised) + [onehot_ref[...]], axis=0).astype(jnp.bfloat16)
    product = lax.dot_general(
        stacked, head_ref[...], (((1,), (1,)), ((), ())), preferred_element_type=jnp.float32
    )
    grad_parts[me, :imgs, :full_width] = (
        product[:imgs] + product[imgs : 2 * imgs] + product[2 * imgs : 3 * imgs]
    )
    grad_parts[me, imgs:, :full_width] = product[3 * imgs :]
    grad_parts[me, :imgs, full_width:] = jnp.broadcast_to(row_max, (imgs, 128))
    grad_parts[me, imgs:, full_width:] = jnp.broadcast_to(row_total, (imgs, 128))
    exchange(grad_parts, 1)
    tops = [grad_parts[source, :imgs, full_width:][:, :1] for source in range(shards)]
    totals = [grad_parts[source, imgs:, full_width:][:, :1] for source in range(shards)]
    top = tops[0]
    for other in tops[1:]:
        top = jnp.maximum(top, other)
    factors = [jnp.exp(one - top) for one in tops]
    total = sum(factor * one for factor, one in zip(factors, totals))
    norm_grad = jnp.zeros((imgs, full_width), jnp.float32)
    for source in range(shards):
        norm_grad = norm_grad + (
            grad_parts[source, :imgs, :full_width] * (factors[source] / total)
            - grad_parts[source, imgs:, :full_width]
        )
    gain_grad = norm_grad * gain
    pool_full = inv_std * (
        gain_grad
        - jnp.mean(gain_grad, axis=-1, keepdims=True)
        - unit_rows * jnp.mean(gain_grad * unit_rows, axis=-1, keepdims=True)
    )
    pool_grad = (pool_full / tok_count).astype(jnp.bfloat16)
    pool_grad_ref[...] = pool_grad
    out_grad_ref[...] = lax.dot_general(
        pool_grad, proj_ref[...], (((1,), (1,)), ((), ())), preferred_element_type=jnp.float32
    ).astype(jnp.bfloat16)


def classify(tok_count, out_sum, x_sum, proj_local, head_local, onehot, head_gain):
    imgs, full_width = x_sum.shape
    shards = lax.axis_size("tp")
    return pl.pallas_call(
        partial(head_kernel, tok_count),
        out_shape=[
            jax.ShapeDtypeStruct((imgs, full_width), jnp.bfloat16),
            jax.ShapeDtypeStruct(out_sum.shape, jnp.bfloat16),
        ],
        in_specs=[pl.BlockSpec(memory_space=pltpu.VMEM)] * 6,
        out_specs=[pl.BlockSpec(memory_space=pltpu.VMEM)] * 2,
        scratch_shapes=[
            pltpu.VMEM((shards, imgs, full_width), jnp.float32),
            pltpu.VMEM((shards, 2 * imgs, full_width + 128), jnp.float32),
            pltpu.SemaphoreType.DMA((2, shards)),
            pltpu.SemaphoreType.DMA((2, shards)),
        ],
        compiler_params=pltpu.CompilerParams(
            collective_id=1, has_side_effects=True, vmem_limit_bytes=32 * 1024 * 1024
        ),
    )(out_sum, x_sum, proj_local, head_local, onehot, head_gain[None])


def on_device(
    activations,
    qkv_weight,
    proj_weight,
    qkv_momentum,
    proj_momentum,
    head_weight,
    labels,
    norm_gain,
    head_gain,
    gossip_round,
):
    local_acts = activations[0]
    img_count, tok_count = (local_acts.shape[0], local_acts.shape[1])
    weight_shard_here = qkv_weight[0]
    local_feats = weight_shard_here.shape[2]
    full_width = weight_shard_here.shape[1]
    normed, qkv, lse, weight_sum, out_sum, x_sum = forward(
        local_acts, weight_shard_here, norm_gain
    )
    out_sum = out_sum.reshape(img_count, local_feats)
    x_sum = x_sum.reshape(img_count, full_width)
    proj_local = proj_weight[0]
    head_local = head_weight[0]
    local_classes = head_local.shape[1]
    class_start = lax.axis_index("tp") * local_classes
    onehot = (
        labels[0][:, None] == class_start + jnp.arange(local_classes, dtype=jnp.int32)[None, :]
    ).astype(jnp.float32)
    pool_grad, out_grad = classify(
        tok_count, out_sum, x_sum, proj_local, head_local, onehot, head_gain
    )
    proj_grad = jnp.dot(out_sum.T, pool_grad.astype(jnp.float32), precision=lax.Precision.HIGHEST)
    proj_new = MOMENTUM * proj_momentum[0] + proj_grad
    proj_step = (proj_local.astype(jnp.float32) - LEARNING_RATE * proj_new).astype(jnp.bfloat16)
    value_grad = (weight_sum * out_grad.astype(jnp.float32)[:, None, :]).astype(jnp.bfloat16)
    value_new, value_step = stepped(normed, value_grad, qkv_momentum[0, 2], weight_shard_here[2])

    def rest(operands, below, above):
        normed, qkv, lse, out_grad, momentum, weight, proj_step, value_step = operands

        def averaged(step):
            return average(
                step, from_behind(step, "rep", below), from_behind(step, "rep", -above)
            )

        proj_avg = averaged(proj_step)
        value_avg = averaged(value_step)
        grads = backward(tok_count, qkv, lse, out_grad)
        key_new, key_step = stepped(normed, grads[1], momentum[1], weight[1])
        key_avg = averaged(key_step)
        query_new, query_step = stepped(normed, grads[0], momentum[0], weight[0])
        query_avg = averaged(query_step)
        return (query_avg, key_avg, value_avg, proj_avg, query_new, key_new)

    query_avg, key_avg, value_avg, proj_avg, query_new, key_new = gossiped(
        rest,
        (
            normed,
            qkv,
            lse,
            out_grad,
            qkv_momentum[0],
            weight_shard_here,
            proj_step,
            value_step,
        ),
        gossip_round,
    )
    return (
        jnp.stack([query_avg, key_avg, value_avg])[None],
        proj_avg[None],
        jnp.stack([query_new, key_new, value_new])[None],
        proj_new[None],
    )


def solution(mesh):
    return jax.shard_map(
        on_device,
        mesh=mesh,
        in_specs=(
            P("rep", None, None, "tp"),
            P("rep", None, None, "tp"),
            P("rep", "tp", None),
            P("rep", None, None, "tp"),
            P("rep", "tp", None),
            P("rep", None, "tp"),
            P("rep", None),
            P(),
            P(),
            P(),
        ),
        out_specs=(
            P("rep", None, None, "tp"),
            P("rep", "tp", None),
            P("rep", None, None, "tp"),
            P("rep", "tp", None),
        ),
        check_vma=False,
    )
```

```python
from functools import partial

import jax
import jax.numpy as jnp
from jax import lax
from jax.experimental import pallas as pl
from jax.experimental.pallas import tpu as pltpu
from jax.sharding import PartitionSpec as P

HEAD_DIM = 80


EPSILON = 1e-06
MOMENTUM = 0.9
LEARNING_RATE = 0.1


def from_behind(block, axis, distance):
    devices = range(lax.axis_size(axis))
    route = [((i - distance) % len(devices), i) for i in devices]
    return lax.ppermute(block, axis, route)


def normalize(values, gain):
    average_row = jnp.mean(values, axis=-1, keepdims=True)
    centred = values - average_row
    broadcast_copies = jnp.mean(centred * centred, axis=-1, keepdims=True)
    inv_std = lax.rsqrt(broadcast_copies + EPSILON)
    unit_rows = centred * inv_std
    return (unit_rows * gain, unit_rows, inv_std)


def average(own_value, from_below, from_above):
    return (
        (
            from_below.astype(jnp.float32)
            + own_value.astype(jnp.float32)
            + from_above.astype(jnp.float32)
        )
        / 3.0
    ).astype(jnp.bfloat16)


def gossiped(work, operands, gossip_round):
    count = lax.axis_size("rep").bit_length() - 1
    branches = [
        partial(work, below=1 << first, above=1 << second)
        for first in range(count)
        for second in range(count)
        if second != first
    ]
    first, second = gossip_round[0], gossip_round[1]
    index = first * (count - 1) + second - (second > first).astype(jnp.int32)
    return lax.switch(index, branches, operands)


def stepped(normed, grad, momentum, weight):
    product = jnp.einsum("sbiw,bil->swl", normed, grad, preferred_element_type=jnp.float32)
    new = MOMENTUM * momentum + product.reshape(momentum.shape)
    return new, (weight.astype(jnp.float32) - LEARNING_RATE * new).astype(jnp.bfloat16)


def head_mask(head, shape):
    lane = lax.broadcasted_iota(jnp.int32, shape, 1)
    return (lane >= head * HEAD_DIM) & (lane < (head + 1) * HEAD_DIM)


def scores_by_key(queries, key_rows, head):
    picked = jnp.where(head_mask(head, queries.shape), queries, jnp.zeros_like(queries))
    return lax.dot_general(
        key_rows, picked, (((1,), (1,)), ((), ())), preferred_element_type=jnp.float32
    ) * (HEAD_DIM ** (-0.5))


def forward_kernel(
    tok_count,
    x_ref,
    w_ref,
    gain_ref,
    normed_ref,
    qkv_ref,
    lse_ref,
    weight_sum_ref,
    out_sum_ref,
    x_sum_ref,
    tokens,
    send_sem,
    pass_sem,
    recv_sem,
):
    shards = tokens.shape[0]
    pairs = tokens.shape[1]
    rows = tokens.shape[3]
    local_feats = x_ref.shape[2]
    local_heads = local_feats // HEAD_DIM
    full_width = shards * local_feats
    me = lax.axis_index("tp")

    barrier = pltpu.get_barrier_semaphore()
    for step in range(1, shards):
        pl.semaphore_signal(
            barrier,
            inc=1,
            device_id={"tp": lax.rem(me + step, shards)},
            device_id_type=pl.DeviceIdType.MESH,
        )
    pl.semaphore_wait(barrier, shards - 1)

    def copy_of(source, pair, target, sem):
        return pltpu.make_async_remote_copy(
            src_ref=tokens.at[source, pair],
            dst_ref=tokens.at[source, pair],
            send_sem=sem,
            recv_sem=recv_sem.at[source, pair],
            device_id={"tp": target},
            device_id_type=pl.DeviceIdType.MESH,
        )

    def send(pair):
        even = x_ref[2 * pair]
        odd = x_ref[2 * pair + 1]
        tokens[me, pair, 0] = even[:, :128]
        tokens[me, pair, 1] = even[:, 128:256]
        tokens[me, pair, 2] = odd[:, :128]
        tokens[me, pair, 3] = odd[:, 128:256]
        tokens[me, pair, 4] = jnp.concatenate([even[:, 256:], odd[:, 256:]], axis=1)
        for distance in (2, -2, 1, -1):
            target = me + distance

            @pl.when((target >= 0) & (target < shards))
            def _():
                copy_of(me, pair, target, send_sem.at[distance + 2, pair]).start()

    send(0)
    send(1)
    valid = lax.broadcasted_iota(jnp.int32, (rows, rows), 0) < tok_count
    passer = (me == 1) | (me == 2)
    passed = jnp.where(me == 1, 3, 0)
    passed_to = jnp.where(me == 1, 0, 3)

    def one_pair(pair, carry):
        @pl.when(passer)
        def _():
            copy_of(passed, pair, passed_to, pass_sem.at[pair]).wait_recv()
            copy_of(passed, pair, passed_to, pass_sem.at[pair]).start()

        for source in range(shards):

            @pl.when((source != me) & ~(passer & (source == passed)))
            def _():
                copy_of(source, pair, source, pass_sem.at[pair]).wait_recv()

        @pl.when(pair + 2 < pairs)
        def _():
            send(pair + 2)

        for parity in range(2):
            img = 2 * pair + parity
            parts = []
            for source in range(shards):
                tail = tokens[source, pair, 4]
                parts.append(
                    jnp.concatenate(
                        [
                            tokens[source, pair, 2 * parity],
                            tokens[source, pair, 2 * parity + 1],
                            tail[:, 64 * parity : 64 * parity + 64],
                        ],
                        axis=1,
                    ).astype(jnp.float32)
                )
            average_row = sum(jnp.sum(part, axis=1, keepdims=True) for part in parts) / full_width
            spread = (
                sum(
                    jnp.sum((part - average_row) * (part - average_row), axis=1, keepdims=True)
                    for part in parts
                )
                / full_width
            )
            inv_std = lax.rsqrt(spread + EPSILON)
            projected = [None] * 3
            for source in range(shards):
                normed = ((parts[source] - average_row) * inv_std * gain_ref[source]).astype(
                    jnp.bfloat16
                )
                normed_ref[source, img] = normed
                x_sum_ref[img, source] = jnp.sum(parts[source], axis=0, keepdims=True)
                for kind in range(3):
                    piece = jnp.dot(
                        normed,
                        w_ref[kind, source * local_feats : (source + 1) * local_feats, :],
                        preferred_element_type=jnp.float32,
                    )
                    projected[kind] = piece if source == 0 else projected[kind] + piece
            queries, key_rows, value_rows = [part.astype(jnp.bfloat16) for part in projected]
            qkv_ref[0, img] = queries
            qkv_ref[1, img] = key_rows
            qkv_ref[2, img] = value_rows
            weight_sum = jnp.zeros((rows, local_feats), jnp.float32)
            token = lax.broadcasted_iota(jnp.int32, (rows, local_feats), 0) < tok_count
            for head in range(local_heads):
                scores = scores_by_key(queries, key_rows, head)
                scores = jnp.where(valid, scores, -1e30)
                top = jnp.max(scores, axis=0, keepdims=True)
                raised = jnp.exp(scores - top)
                total = jnp.sum(raised, axis=0, keepdims=True)
                attend = (raised / total).astype(jnp.bfloat16)
                lse_ref[img, head : head + 1] = top + jnp.log(total)
                picked = (token & head_mask(head, (rows, local_feats))).astype(jnp.bfloat16)
                weight_sum = weight_sum + jnp.dot(
                    attend, picked, preferred_element_type=jnp.float32
                )
            weight_sum_ref[img] = weight_sum
            out_sum_ref[img] = jnp.sum(
                weight_sum * value_rows.astype(jnp.float32), axis=0, keepdims=True
            )
        return carry

    lax.fori_loop(0, pairs, one_pair, 0)

    def finish(pair, carry):
        for distance in (2, -2, 1, -1):
            target = me + distance

            @pl.when((target >= 0) & (target < shards))
            def _():
                copy_of(me, pair, target, send_sem.at[distance + 2, pair]).wait_send()

        @pl.when(passer)
        def _():
            copy_of(passed, pair, passed_to, pass_sem.at[pair]).wait_send()

        return carry

    lax.fori_loop(0, pairs, finish, 0)


def forward(local_acts, weight_shard, norm_gain):
    img_count, tok_count, local_feats = local_acts.shape
    shards = lax.axis_size("tp")
    rows = -(-tok_count // 16) * 16
    pairs = img_count // 2
    padded = jnp.pad(local_acts, ((0, 0), (0, rows - tok_count), (0, 0)))
    gain = norm_gain.reshape(shards, 1, local_feats)
    shapes = [
        jax.ShapeDtypeStruct((shards, img_count, rows, local_feats), jnp.bfloat16),
        jax.ShapeDtypeStruct((3, img_count, rows, local_feats), jnp.bfloat16),
        jax.ShapeDtypeStruct((img_count, 8, rows), jnp.float32),
        jax.ShapeDtypeStruct((img_count, rows, local_feats), jnp.float32),
        jax.ShapeDtypeStruct((img_count, 1, local_feats), jnp.float32),
        jax.ShapeDtypeStruct((img_count, shards, 1, local_feats), jnp.float32),
    ]
    return pl.pallas_call(
        partial(forward_kernel, tok_count),
        out_shape=shapes,
        in_specs=[pl.BlockSpec(memory_space=pltpu.VMEM)] * 3,
        out_specs=[pl.BlockSpec(memory_space=pltpu.VMEM)] * len(shapes),
        scratch_shapes=[
            pltpu.VMEM((shards, pairs, 5, rows, 128), jnp.bfloat16),
            pltpu.SemaphoreType.DMA((5, pairs)),
            pltpu.SemaphoreType.DMA((pairs,)),
            pltpu.SemaphoreType.DMA((shards, pairs)),
        ],
        compiler_params=pltpu.CompilerParams(
            collective_id=0, has_side_effects=True, vmem_limit_bytes=56 * 1024 * 1024
        ),
    )(padded, weight_shard, gain)


def backward_kernel(tok_count, qkv_ref, lse_ref, out_grad_ref, grad_ref):
    queries, key_rows, value_rows = qkv_ref[0, 0], qkv_ref[1, 0], qkv_ref[2, 0]
    rows, local_feats = queries.shape
    local_heads = local_feats // HEAD_DIM
    out_grad = out_grad_ref[0].astype(jnp.float32)
    valid = lax.broadcasted_iota(jnp.int32, (rows, rows), 0) < tok_count
    weighed = value_rows.astype(jnp.float32) * out_grad

    def one_head(head, carry):
        query_grad, key_grad = carry
        mask = head_mask(head, (rows, local_feats))
        scores = scores_by_key(queries, key_rows, head)
        attend = jnp.where(valid, jnp.exp(scores - lse_ref[0, pl.ds(head, 1)]), 0.0)
        value_dot = jnp.sum(jnp.where(mask, weighed, 0.0), axis=1, keepdims=True)
        row_dot = jnp.sum(attend * value_dot, axis=0, keepdims=True)
        score_grad = (attend * (value_dot - row_dot)).astype(jnp.bfloat16)
        key_grad = key_grad + jnp.dot(
            score_grad,
            jnp.where(mask, queries, jnp.zeros_like(queries)),
            preferred_element_type=jnp.float32,
        )
        query_grad = query_grad + lax.dot_general(
            score_grad,
            jnp.where(mask, key_rows, jnp.zeros_like(key_rows)),
            (((0,), (0,)), ((), ())),
            preferred_element_type=jnp.float32,
        )
        return query_grad, key_grad

    zeros = jnp.zeros((rows, local_feats), jnp.float32)
    query_grad, key_grad = lax.fori_loop(0, local_heads, one_head, (zeros, zeros))
    scale = HEAD_DIM ** (-0.5)
    grad_ref[0, 0] = (query_grad * scale).astype(jnp.bfloat16)
    grad_ref[1, 0] = (key_grad * scale).astype(jnp.bfloat16)


def backward(tok_count, qkv, lse, out_grad):
    _, img_count, rows, local_feats = qkv.shape
    return pl.pallas_call(
        partial(backward_kernel, tok_count),
        grid=(img_count,),
        out_shape=jax.ShapeDtypeStruct((2,) + qkv.shape[1:], jnp.bfloat16),
        in_specs=[
            pl.BlockSpec((3, 1, rows, local_feats), lambda i: (0, i, 0, 0)),
            pl.BlockSpec((1, 8, rows), lambda i: (i, 0, 0)),
            pl.BlockSpec((1, 1, local_feats), lambda i: (i, 0, 0)),
        ],
        out_specs=pl.BlockSpec((2, 1, rows, local_feats), lambda i: (0, i, 0, 0)),
        cost_estimate=pl.CostEstimate(
            flops=20_000_000_000, bytes_accessed=16_000_000, transcendentals=4_000_000
        ),
        compiler_params=pltpu.CompilerParams(vmem_limit_bytes=48 * 1024 * 1024),
    )(qkv, lse, out_grad[:, None])


def thirds(values):
    high = values.astype(jnp.bfloat16).astype(jnp.float32)
    middle = (values - high).astype(jnp.bfloat16).astype(jnp.float32)
    return [high, middle, values - high - middle]


def head_kernel(
    tok_count,
    out_sum_ref,
    x_sum_ref,
    proj_ref,
    head_ref,
    onehot_ref,
    gain_ref,
    pool_grad_ref,
    out_grad_ref,
    pooled_parts,
    grad_parts,
    send_sem,
    recv_sem,
):
    shards = pooled_parts.shape[0]
    imgs, full_width = x_sum_ref.shape
    me = lax.axis_index("tp")

    barrier = pltpu.get_barrier_semaphore()
    for step in range(1, shards):
        pl.semaphore_signal(
            barrier,
            inc=1,
            device_id={"tp": lax.rem(me + step, shards)},
            device_id_type=pl.DeviceIdType.MESH,
        )

    def exchange(parts, turn):
        copies = [
            pltpu.make_async_remote_copy(
                src_ref=parts.at[me],
                dst_ref=parts.at[me],
                send_sem=send_sem.at[turn, step],
                recv_sem=recv_sem.at[turn, step],
                device_id={"tp": lax.rem(me + step, shards)},
                device_id_type=pl.DeviceIdType.MESH,
            )
            for step in range(1, shards)
        ]
        for copy in copies:
            copy.start()
        for copy in copies:
            copy.wait()

    split = jnp.concatenate(thirds(out_sum_ref[...]), axis=0).astype(jnp.bfloat16)
    product = jnp.dot(split, proj_ref[...], preferred_element_type=jnp.float32)
    pooled_parts[me] = product[:imgs] + product[imgs : 2 * imgs] + product[2 * imgs :]
    pl.semaphore_wait(barrier, shards - 1)
    exchange(pooled_parts, 0)
    pooled = x_sum_ref[...]
    for source in range(shards):
        pooled = pooled + pooled_parts[source]
    pooled = pooled / tok_count
    gain = gain_ref[...]
    scaled, unit_rows, inv_std = normalize(pooled, gain)
    logits = jnp.dot(
        scaled.astype(jnp.bfloat16), head_ref[...], preferred_element_type=jnp.float32
    )
    row_max = jnp.max(logits, axis=1, keepdims=True)
    raised = jnp.exp(logits - row_max)
    row_total = jnp.sum(raised, axis=1, keepdims=True)
    stacked = jnp.concatenate(thirds(raised) + [onehot_ref[...]], axis=0).astype(jnp.bfloat16)
    product = lax.dot_general(
        stacked, head_ref[...], (((1,), (1,)), ((), ())), preferred_element_type=jnp.float32
    )
    grad_parts[me, :imgs, :full_width] = (
        product[:imgs] + product[imgs : 2 * imgs] + product[2 * imgs : 3 * imgs]
    )
    grad_parts[me, imgs:, :full_width] = product[3 * imgs :]
    grad_parts[me, :imgs, full_width:] = jnp.broadcast_to(row_max, (imgs, 128))
    grad_parts[me, imgs:, full_width:] = jnp.broadcast_to(row_total, (imgs, 128))
    exchange(grad_parts, 1)
    tops = [grad_parts[source, :imgs, full_width:][:, :1] for source in range(shards)]
    totals = [grad_parts[source, imgs:, full_width:][:, :1] for source in range(shards)]
    top = tops[0]
    for other in tops[1:]:
        top = jnp.maximum(top, other)
    factors = [jnp.exp(one - top) for one in tops]
    total = sum(factor * one for factor, one in zip(factors, totals))
    norm_grad = jnp.zeros((imgs, full_width), jnp.float32)
    for source in range(shards):
        norm_grad = norm_grad + (
            grad_parts[source, :imgs, :full_width] * (factors[source] / total)
            - grad_parts[source, imgs:, :full_width]
        )
    gain_grad = norm_grad * gain
    pool_full = inv_std * (
        gain_grad
        - jnp.mean(gain_grad, axis=-1, keepdims=True)
        - unit_rows * jnp.mean(gain_grad * unit_rows, axis=-1, keepdims=True)
    )
    pool_grad = (pool_full / tok_count).astype(jnp.bfloat16)
    pool_grad_ref[...] = pool_grad
    out_grad_ref[...] = lax.dot_general(
        pool_grad, proj_ref[...], (((1,), (1,)), ((), ())), preferred_element_type=jnp.float32
    ).astype(jnp.bfloat16)


def classify(tok_count, out_sum, x_sum, proj_local, head_local, onehot, head_gain):
    imgs, full_width = x_sum.shape
    shards = lax.axis_size("tp")
    return pl.pallas_call(
        partial(head_kernel, tok_count),
        out_shape=[
            jax.ShapeDtypeStruct((imgs, full_width), jnp.bfloat16),
            jax.ShapeDtypeStruct(out_sum.shape, jnp.bfloat16),
        ],
        in_specs=[pl.BlockSpec(memory_space=pltpu.VMEM)] * 6,
        out_specs=[pl.BlockSpec(memory_space=pltpu.VMEM)] * 2,
        scratch_shapes=[
            pltpu.VMEM((shards, imgs, full_width), jnp.float32),
            pltpu.VMEM((shards, 2 * imgs, full_width + 128), jnp.float32),
            pltpu.SemaphoreType.DMA((2, shards)),
            pltpu.SemaphoreType.DMA((2, shards)),
        ],
        compiler_params=pltpu.CompilerParams(
            collective_id=1, has_side_effects=True, vmem_limit_bytes=32 * 1024 * 1024
        ),
    )(out_sum, x_sum, proj_local, head_local, onehot, head_gain[None])


def on_device(
    activations,
    qkv_weight,
    proj_weight,
    qkv_momentum,
    proj_momentum,
    head_weight,
    labels,
    norm_gain,
    head_gain,
    gossip_round,
):
    local_acts = activations[0]
    img_count, tok_count = (local_acts.shape[0], local_acts.shape[1])
    weight_shard_here = qkv_weight[0]
    local_feats = weight_shard_here.shape[2]
    full_width = weight_shard_here.shape[1]
    normed, qkv, lse, weight_sum, out_sum, x_sum = forward(
        local_acts, weight_shard_here, norm_gain
    )
    out_sum = out_sum.reshape(img_count, local_feats)
    x_sum = x_sum.reshape(img_count, full_width)
    proj_local = proj_weight[0]
    head_local = head_weight[0]
    local_classes = head_local.shape[1]
    class_start = lax.axis_index("tp") * local_classes
    onehot = (
        labels[0][:, None] == class_start + jnp.arange(local_classes, dtype=jnp.int32)[None, :]
    ).astype(jnp.float32)
    pool_grad, out_grad = classify(
        tok_count, out_sum, x_sum, proj_local, head_local, onehot, head_gain
    )
    proj_grad = jnp.dot(out_sum.T, pool_grad.astype(jnp.float32), precision=lax.Precision.HIGHEST)
    proj_new = MOMENTUM * proj_momentum[0] + proj_grad
    proj_step = (proj_local.astype(jnp.float32) - LEARNING_RATE * proj_new).astype(jnp.bfloat16)
    value_grad = (weight_sum * out_grad.astype(jnp.float32)[:, None, :]).astype(jnp.bfloat16)
    value_new, value_step = stepped(normed, value_grad, qkv_momentum[0, 2], weight_shard_here[2])

    def rest(operands, below, above):
        normed, qkv, lse, out_grad, momentum, weight, proj_step, value_step = operands

        def averaged(step):
            return (step, from_behind(step, "rep", below), from_behind(step, "rep", -above))

        proj_avg = averaged(proj_step)
        value_avg = averaged(value_step)
        grads = backward(tok_count, qkv, lse, out_grad)
        key_new, key_step = stepped(normed, grads[1], momentum[1], weight[1])
        key_avg = averaged(key_step)
        query_new, query_step = stepped(normed, grads[0], momentum[0], weight[0])
        query_avg = averaged(query_step)
        return (query_avg, key_avg, value_avg, proj_avg, query_new, key_new)

    query_avg, key_avg, value_avg, proj_avg, query_new, key_new = gossiped(
        rest,
        (
            normed,
            qkv,
            lse,
            out_grad,
            qkv_momentum[0],
            weight_shard_here,
            proj_step,
            value_step,
        ),
        gossip_round,
    )
    return (
        jnp.stack([average(*query_avg), average(*key_avg), average(*value_avg)])[None],
        average(*proj_avg)[None],
        jnp.stack([query_new, key_new, value_new])[None],
        proj_new[None],
    )


def solution(mesh):
    return jax.shard_map(
        on_device,
        mesh=mesh,
        in_specs=(
            P("rep", None, None, "tp"),
            P("rep", None, None, "tp"),
            P("rep", "tp", None),
            P("rep", None, None, "tp"),
            P("rep", "tp", None),
            P("rep", None, "tp"),
            P("rep", None),
            P(),
            P(),
            P(),
        ),
        out_specs=(
            P("rep", None, None, "tp"),
            P("rep", "tp", None),
            P("rep", None, None, "tp"),
            P("rep", "tp", None),
        ),
        check_vma=False,
    )
```
